1024 devices in a mesh: dp: 16 (over y, x_hi), fsdp: 64 (over x_lo, z, core).
Axes of the slice: x: 4 (x_hi: 2, x_lo: 2; x = x_hi * 2 + x_lo), y: 8, z: 16, core: 2. Of those that a mesh axis runs over, the one named last changes fastest.
Arguments:
- attn_out: bfloat16 [18432, 4096], P('fsdp', 'dp'), may hold values from -6 to 6
- residual: bfloat16 [18432, 4096], P('fsdp', 'dp'), may hold values from -32 to 32
- out_proj: bfloat16 [4096, 4096], P('fsdp', 'dp'), may hold values from -0.09375 to 0.09375
- gain: float32 [4096], P('dp'), may hold values from 0.3 to 3
- positives: int32 [6144], P('fsdp'), may hold values from 0 to 191
Outputs:
- logits: float32 [6144, 192], P('fsdp')
- dlogits: float32 [6144, 192], P('fsdp')
- d_attn: bfloat16 [18432, 4096], P('fsdp', 'dp')
- d_resid: float32 [18432, 4096], P('fsdp', 'dp')
The draws below stay inside these ranges and needn't reach their ends.
All inputs are finite; a program needn't handle non-finite values.
Results may differ from the reference program's by a relative error of at most 0.02.
Values may be sent and summed in bfloat16 or wider, within the bound.
A program may use at most 32 MiB of HBM per device.

```python
import math
import jax
import jax.numpy as jnp
from jax import lax

D = 4096
QRY = 96
PSG = 192
GROUP = 288
ROWS = 18432
N_DP = 16
N_FSDP = 64


def draw_residual(key, part):
    key = jax.random.fold_in(key, 11)
    key_rows, key_base = jax.random.split(key, 2)
    row_scale = jnp.exp(jax.random.uniform(key_rows, (ROWS, 1), jnp.float32, 0.0, math.log(8.0)))
    base = jnp.clip(jax.random.normal(key_base, (ROWS, D), jnp.float32), -4.0, 4.0)
    return (base * row_scale).astype(jnp.bfloat16)


def place_ends(array, key, smallest, high):
    extent = array.shape
    spot = [jax.random.randint(jax.random.fold_in(key, axis), (), 0, extent[axis]) for axis in range(len(extent))]
    array = array.at[tuple(spot)].set(smallest)
    longest = extent.index(max(extent))
    spot[longest] = (spot[longest] + 1) % extent[longest]
    return array.at[tuple(spot)].set(high)


def shard_levels(key, dims, cuts, low, high):
    def one(axis_at, shards_of):
        draws = jax.random.uniform(jax.random.fold_in(jax.random.fold_in(key, 6), axis_at), (shards_of,), jnp.float32, low / len(cuts), high / len(cuts))
        return jnp.repeat(jnp.exp(draws), dims[axis_at] // shards_of).reshape((-1,) + (1,) * (len(dims) - axis_at - 1))

    loudness = one(*cuts[0])
    for cut in cuts[1:]:
        loudness = loudness * one(*cut)
    return loudness


def bell_draw(key, shape, spread, most, pieces=(), dtype=jnp.bfloat16):
    factor_of = shard_levels(key, shape, pieces, -0.22, 0.18) if pieces else 1.0
    result = jax.random.normal(key, shape, jnp.float32) * spread * factor_of
    return jnp.minimum(jnp.maximum(result, -most), most).astype(dtype)


def setup_inputs(seed: int = 0) -> dict:
    splits = jax.random.split(jax.random.key(seed), 6)
    return {
        "attn_out": bell_draw(splits[0], (ROWS, D), 1.0, 6.0, ((0, 64), (1, 16))),
        "residual": draw_residual(jax.random.fold_in(splits[5], 71), 0),
        "out_proj": bell_draw(splits[2], (D, D), D ** -0.5, 0.09375, ((0, 64), (1, 16))),
        "gain": jnp.clip(jnp.exp(math.log(3.0) - 2.3025851 * jax.random.uniform(splits[3], (D,), jnp.float32) ** shard_levels(splits[3], (D,), ((0, 16),), -0.2, 0.2)), 0.3, 3.0),
        "positives": place_ends(jax.random.randint(splits[4], (QRY * N_FSDP,), 0, PSG), jax.random.fold_in(splits[4], 1), 0, PSG - 1).astype(jnp.int32),
    }


logit_scale = 20.0
loss_scale = 1024.0
highest = lax.Precision.HIGHEST

def group_pass(attn_rows, resid_rows, positive_rows, out_proj, gain):
    mixed = jnp.dot(attn_rows, out_proj, preferred_element_type=jnp.float32)
    scaled = (resid_rows.astype(jnp.float32) + mixed) * gain[None, :]
    norms = jnp.sqrt(lax.optimization_barrier(jnp.sum(scaled * scaled, axis=1)) + 1e-06)
    unit = scaled / norms[:, None]
    unit_q = unit[:QRY]
    unit_p = unit[QRY:]
    logits = logit_scale * jnp.dot(unit_q, unit_p.T, precision=highest)
    shifted = jnp.exp(logits - logit_scale)
    probs = shifted / lax.optimization_barrier(jnp.sum(shifted, axis=1, keepdims=True))
    target = (positive_rows[:, None] == lax.broadcasted_iota(jnp.int32, probs.shape, 1)).astype(jnp.float32)
    dlogits = probs - target
    weighted = dlogits * logits
    grad_q = (logit_scale * jnp.dot(dlogits, unit_p, precision=highest) - lax.optimization_barrier(jnp.sum(weighted, axis=1))[:, None] * unit_q) / norms[:QRY, None]
    grad_p = (logit_scale * jnp.dot(dlogits.T, unit_q, precision=highest) - lax.optimization_barrier(jnp.sum(weighted, axis=0))[:, None] * unit_p) / norms[QRY:, None]
    d_resid = loss_scale * gain[None, :] * jnp.concatenate([grad_q, grad_p], axis=0)
    d_mixed = d_resid.astype(jnp.bfloat16)
    width = D // N_DP
    blocks = d_mixed.astype(jnp.float32).reshape(GROUP, N_DP, width)
    weights = out_proj.astype(jnp.float32).reshape(D, N_DP, width)
    partials = jnp.einsum('gcw,dcw->cgd', blocks, weights, precision=highest).astype(jnp.bfloat16)
    partials = lax.optimization_barrier(partials)
    d_attn = lax.optimization_barrier(jnp.sum(partials.astype(jnp.float32), axis=0)).astype(jnp.bfloat16)
    return (logits, dlogits, d_attn, d_resid)

def reference(attn_out, residual, out_proj, gain, positives):
    attn_groups = attn_out.reshape(N_FSDP, GROUP, D)
    resid_groups = residual.reshape(N_FSDP, GROUP, D)
    positive_groups = positives.reshape(N_FSDP, QRY)

    def one_group(items):
        return group_pass(items[0], items[1], items[2], out_proj, gain)
    logits, dlogits, d_attn, d_resid = lax.map(one_group, (attn_groups, resid_groups, positive_groups))
    return (logits.reshape(N_FSDP * QRY, PSG), dlogits.reshape(N_FSDP * QRY, PSG), d_attn.reshape(ROWS, D), d_resid.reshape(ROWS, D))
```

```python
import jax
import jax.numpy as jnp
from jax import lax
from jax.experimental import pallas as pl
from jax.experimental.pallas import tpu as pltpu
from jax.sharding import PartitionSpec as P

QRY = 96
PSG = 192
GROUP = 288
W = 256
NY, NZ = 8, 16
ROWS_X = 128
ROWS_Y = GROUP - ROWS_X
SLICES = QRY // 8

logit_scale = 20.0
loss_scale = 1024.0
highest = lax.Precision.HIGHEST
f32 = jnp.float32
bf16 = jnp.bfloat16
MESH = pl.DeviceIdType.MESH


def device(y, h, l, z, k):
    return (y * 2 + h, l * 32 + z * 2 + k)


def dot_t(left, right, precision=None):
    return lax.dot_general(
        left, right, (((1,), (1,)), ((), ())), precision=precision, preferred_element_type=f32
    )


def remote(src, dst, send, recv, target):
    return pltpu.make_async_remote_copy(
        src_ref=src, dst_ref=dst, send_sem=send, recv_sem=recv, device_id=target, device_id_type=MESH
    )


ROWS = {"a": (0, ROWS_X), "p": (0, ROWS_X), "b": (ROWS_X, ROWS_Y)}


def rows_of(kind, hop, way):
    start, size = ROWS[kind]
    if hop < 3:
        return start, size
    return start + way * (size // 2), size // 2


def main_kernel(
    attn_hbm, resid_hbm, weight_hbm, gain,
    t_out, scaled_out, z_out,
    g, wp, t, so, sp, ro, rp, xs, xr, ps, pr, zpart, zin, zsum,
    ag_s, ag_r, ax_s, ax_r, bx_s, bx_r, wl_s, wl_r, wz_s, wz_r, wk_s, wk_r,
    rs_s, rs_r, rx_s, rx_r, rp_s, rp_r, z1_s, z1_r, z2_s, z2_r,
    resid, in_sem,
):
    c = lax.axis_index("dp")
    f = lax.axis_index("fsdp")
    y, h = c // 2, c % 2
    l, z, k = f // 32, (f // 2) % 16, f % 2
    across = device(y, 1 - h, l, z, k)
    beside = device(y, h, 1 - l, z, k)
    sibling = device(y, h, l, z, 1 - k)
    along = (device((y + 1) % NY, h, l, z, k), device((y + NY - 1) % NY, h, l, z, k))
    z_near = (device(y, h, l, (z + 1) % NZ, k), device(y, h, l, (z + NZ - 1) % NZ, k))
    z_far = (device(y, h, l, (z + 2) % NZ, k), device(y, h, l, (z + NZ - 2) % NZ, k))
    peers = [((c + r) % 16, f) for r in range(1, 16)]

    barrier = pltpu.get_barrier_semaphore()
    everyone = peers + [beside, sibling, *z_near, *z_far]
    for target in everyone:
        pl.semaphore_signal(barrier, inc=1, device_id=target, device_id_type=MESH)
    load_a = pltpu.make_async_copy(attn_hbm, g.at[c], in_sem.at[0])
    load_w = pltpu.make_async_copy(weight_hbm, wp.at[l, z, k], in_sem.at[1])
    load_r = pltpu.make_async_copy(resid_hbm, resid, in_sem.at[2])
    load_a.start()
    load_w.start()
    load_r.start()
    load_a.wait()
    load_w.wait()
    load_r.wait()
    pl.semaphore_wait(barrier, len(everyone))

    def slot(step, other=0):
        return ((y + step + NY) % NY) * 2 + (1 - h if other else h)

    KINDS = ("a", "b", "p")

    def ag(kind, way, hop):
        start, size = rows_of(kind, hop, way)
        block = g.at[slot(-hop if way == 0 else hop, kind == "p"), pl.ds(start, size)]
        i = KINDS.index(kind)
        return remote(block, block, ag_s.at[i, way, hop], ag_r.at[i, way, hop], along[way])

    def ag_recv(kind, way, hop):
        start, size = rows_of(kind, hop, way)
        block = g.at[slot(-hop - 1 if way == 0 else hop + 1, kind == "p"), pl.ds(start, size)]
        i = KINDS.index(kind)
        return remote(block, block, ag_s.at[i, way, hop], ag_r.at[i, way, hop], along[way])

    def ax(other=0):
        block = g.at[slot(0, other), pl.ds(0, ROWS_X)]
        return remote(block, block, ax_s, ax_r, across)

    steps = [(0, ROWS_X, ROWS_Y)]
    for d in (1, 2, 3):
        steps += [(-d, ROWS_X, ROWS_Y), (d, ROWS_X, ROWS_Y)]
    steps += [(4, ROWS_X, ROWS_Y // 2), (4, ROWS_X + ROWS_Y // 2, ROWS_Y // 2)]

    def bx(i, other=0):
        step, start, size = steps[i]
        block = g.at[slot(step, other), pl.ds(start, size)]
        return remote(block, block, bx_s.at[i], bx_r.at[i], across)

    def wz(u, way, dist):
        hop = 2 if dist % 2 == 0 else 1
        back = dist - hop
        zz = (z - back + NZ) % NZ if way == 0 else (z + back) % NZ
        block = wp.at[1 - l if u else l, zz, k]
        target = (z_far if hop == 2 else z_near)[way]
        return remote(block, block, wz_s.at[u, way, dist - 1], wz_r.at[u, way, dist - 1], target)

    def wz_recv(u, way, dist):
        zz = (z - dist + NZ) % NZ if way == 0 else (z + dist) % NZ
        block = wp.at[1 - l if u else l, zz, k]
        return remote(block, block, wz_s.at[u, way, dist - 1], wz_r.at[u, way, dist - 1], z_near[way])

    def reach(way):
        return 8 if way == 0 else 7

    def wl(u=0):
        block = wp.at[1 - l if u else l, z, k]
        return remote(block, block, wl_s, wl_r, beside)

    def wk(way, dist, core):
        zz = (z - dist + NZ) % NZ if way == 0 else (z + dist) % NZ
        block = wp.at[:, zz, core]
        return remote(block, block, wk_s.at[way, dist], wk_r.at[way, dist], sibling)

    def wz_start(u, way, stage):
        for dist in (2 * stage + 2, 2 * stage + 1):
            if dist <= reach(way):
                wz(u, way, dist).start()

    ax().start()
    wl().start()
    for way in (0, 1):
        ag("a", way, 0).start()
        wz_start(0, way, 0)
        ag("b", way, 0).start()
    bx(0).start()
    wl(1).wait_recv()
    for way in (0, 1):
        wz_start(1, way, 0)
    wk(0, 0, k).start()
    ax(1).wait_recv()
    for way in (0, 1):
        ag("p", way, 0).start()
    for hop in range(4):
        for kind in KINDS:
            for way in (0, 1):
                ag_recv(kind, way, hop).wait_recv()
                if hop < 3:
                    ag(kind, way, hop + 1).start()
                if kind == "b":
                    bx(1 + 2 * hop + way).start()
            if kind == "a":
                u = 0
            elif kind == "p":
                u = 1
            else:
                continue
            for way in (0, 1):
                if 2 * hop + 2 <= reach(way):
                    wz_recv(u, way, 2 * hop + 2).wait_recv()
                    if hop < 3:
                        wz_start(u, way, hop + 1)
        for way in (0, 1):
            for dist in (2 * hop + 1, 2 * hop + 2):
                if dist <= reach(way):
                    if dist % 2:
                        wz_recv(0, way, dist).wait_recv()
                        wz_recv(1, way, dist).wait_recv()
                    wk(way, dist, k).start()
    for i in range(9):
        bx(i, 1).wait_recv()
    wk(0, 0, 1 - k).wait_recv()
    for way in (0, 1):
        for dist in range(1, reach(way) + 1):
            wk(way, dist, 1 - k).wait_recv()

    def panel(index):
        return wp[index // 8, pl.ds(2 * (index % 8), 2)].reshape(W, W)

    total = jnp.dot(g[0], panel(0), preferred_element_type=f32)
    for j in range(1, 16):
        total = total + jnp.dot(g[j], panel(j), preferred_element_type=f32)
    scaled = (resid[...].astype(f32) + total) * gain[...]
    scaled_out[...] = scaled

    queries, passages = scaled[:QRY], scaled[QRY:]
    zpart[:, :PSG] = dot_t(queries, passages, highest)
    squares = jnp.sum(scaled * scaled, axis=1, keepdims=True)
    lane = lax.broadcasted_iota(jnp.int32, (QRY, W - PSG), 1)
    zpart[:, PSG:] = jnp.where(
        lane == 0, squares[:QRY], jnp.where(lane == 1, squares[QRY : 2 * QRY], squares[2 * QRY :])
    )

    def z1(r):
        to = (c + r) % 16
        return to, remote(
            zpart.at[pl.ds(pl.multiple_of(8 * to, 8), 8)], zin.at[c], z1_s.at[r], z1_r.at[r], (to, f)
        )

    for r in range(1, 16):
        to = (c + r) % 16

        @pl.when(to < SLICES)
        def _():
            z1(r)[1].start()

    u = (scaled * gain[...]).astype(bf16)

    def term(step, other):
        index = slot(step, other)
        t[index] = dot_t(u, panel(index))

    def rx(i):
        return remote(xs.at[i], xr.at[i], rx_s.at[i], rx_r.at[i], across)

    order = (4, 3, -3, 2, -2, 1, -1, 0)

    def x_send(step):
        i = order.index(step)
        xs[i] = t[slot(step, 1), ROWS_X:].astype(bf16)
        rx(i).start()

    def rs(kind, way, stage):
        start, size = rows_of(kind, 3 - stage, way)
        if kind == "p":
            src, dst = sp.at[way, stage, pl.ds(start, size)], rp.at[way, stage, pl.ds(start, size)]
        else:
            src, dst = so.at[way, stage, pl.ds(start, size)], ro.at[way, stage, pl.ds(start, size)]
        i = KINDS.index(kind)
        return remote(src, dst, rs_s.at[i, way, stage], rs_r.at[i, way, stage], along[way])

    def own(kind, step, start, size):
        value = t[slot(step, kind == "p"), pl.ds(start, size)]
        if kind == "b":
            value = value + xr[order.index(step), pl.ds(start - ROWS_X, size)].astype(f32)
        return value

    def rs_send(kind, way, stage):
        dist = 4 - stage
        step = 4 if dist == 4 else (dist if way == 0 else -dist)
        out = sp if kind == "p" else so
        start, size = rows_of(kind, 3 - stage, way)
        got = rp if kind == "p" else ro
        if stage == 0:
            out[way, 0, pl.ds(start, size)] = own(kind, step, start, size).astype(bf16)
        elif stage == 1:
            rs(kind, way, 0).wait_recv()
            first, part = rows_of(kind, 3, way)
            rest, _ = rows_of(kind, 3, 1 - way)
            out[way, 1, pl.ds(first, part)] = (
                own(kind, step, first, part) + got[way, 0, pl.ds(first, part)].astype(f32)
            ).astype(bf16)
            out[way, 1, pl.ds(rest, part)] = own(kind, step, rest, part).astype(bf16)
        else:
            rs(kind, way, stage - 1).wait_recv()
            out[way, stage, pl.ds(start, size)] = (
                own(kind, step, start, size) + got[way, stage - 1, pl.ds(start, size)].astype(f32)
            ).astype(bf16)
        rs(kind, way, stage).start()

    for step in order:
        term(step, 1)
        x_send(step)
        term(step, 0)
        if step == 4:
            for kind in ("p", "a"):
                for way in (0, 1):
                    rs_send(kind, way, 0)
    rx(0).wait_recv()
    for way in (0, 1):
        rs_send("b", way, 0)

    def z2(r):
        to = (c + r) % 16
        mine = zsum.at[pl.ds(pl.multiple_of(8 * c, 8), 8)]
        return remote(mine, mine, z2_s.at[r], z2_r.at[r], (to, f))

    for stage in (1, 2, 3):
        for kind in ("p", "a", "b"):
            for way in (0, 1):
                if kind == "b":
                    dist = 4 - stage
                    rx(order.index(dist if way == 0 else -dist)).wait_recv()
                rs_send(kind, way, stage)
        if stage == 1:

            @pl.when(c < SLICES)
            def _():
                for r in range(1, 16):
                    theirs = zin.at[(c + 16 - r) % 16]
                    remote(theirs, theirs, z1_s.at[r], z1_r.at[r], ((c + r) % 16, f)).wait_recv()
                zin[c] = zpart[pl.ds(pl.multiple_of(8 * c, 8), 8)]
                acc = zin[0]
                for j in range(1, 16):
                    acc = acc + zin[j]
                zsum[pl.ds(pl.multiple_of(8 * c, 8), 8)] = acc
                for r in range(1, 16):
                    z2(r).start()

    def landed(kind):
        start, size = ROWS[kind]
        got = rp if kind == "p" else ro
        for way in (0, 1):
            rs(kind, way, 3).wait_recv()
        return (
            own(kind, 0, start, size)
            + got[0, 3, pl.ds(start, size)].astype(f32)
            + got[1, 3, pl.ds(start, size)].astype(f32)
        )

    last = remote(ps, pr, rp_s, rp_r, across)
    ps[...] = landed("p").astype(bf16)
    last.start()
    a_sum = landed("a")
    rx(order.index(0)).wait_recv()
    t_out[ROWS_X:] = landed("b")
    last.wait_recv()
    t_out[:ROWS_X] = a_sum + pr[...].astype(f32)

    for r in range(1, 16):
        by = (c + 16 - r) % 16

        @pl.when(by < SLICES)
        def _():
            theirs = zsum.at[pl.ds(pl.multiple_of(8 * by, 8), 8)]
            remote(theirs, theirs, z2_s.at[r], z2_r.at[r], (by, f)).wait_recv()

    z_out[...] = zsum[...]

    ax().wait_send()
    wl().wait_send()
    for i in range(9):
        bx(i).wait_send()
    for way in (0, 1):
        for hop in range(4):
            for kind in KINDS:
                ag(kind, way, hop).wait_send()
                rs(kind, way, hop).wait_send()
        for dist in range(1, reach(way) + 1):
            wz(0, way, dist).wait_send()
            wz(1, way, dist).wait_send()
            wk(way, dist, k).wait_send()
    wk(0, 0, k).wait_send()
    for i in range(8):
        rx(i).wait_send()
    last.wait_send()
    for r in range(1, 16):

        @pl.when((c + r) % 16 < SLICES)
        def _():
            z1(r)[1].wait_send()

    @pl.when(c < SLICES)
    def _():
        for r in range(1, 16):
            z2(r).wait_send()


def tail_kernel(total, scaled, inner, gain, positives, logits_out, dlogits_out, d_attn, d_resid):
    eye = lax.broadcasted_iota(jnp.int32, (QRY, QRY), 0) == lax.broadcasted_iota(
        jnp.int32, (QRY, QRY), 1
    )

    def as_row(column):
        return jnp.sum(jnp.where(eye, column, 0.0), axis=0, keepdims=True)

    norm_q = jnp.sqrt(inner[:, PSG : PSG + 1] + 1e-06)
    norm_p1 = jnp.sqrt(inner[:, PSG + 1 : PSG + 2] + 1e-06)
    norm_p2 = jnp.sqrt(inner[:, PSG + 2 : PSG + 3] + 1e-06)
    norm_p = jnp.concatenate([norm_p1, norm_p2], axis=0)
    row_p = jnp.concatenate([as_row(norm_p1), as_row(norm_p2)], axis=1)
    logits = logit_scale * inner[:, :PSG] / (norm_q * row_p)
    shifted = jnp.exp(logits - logit_scale)
    probs = shifted / jnp.sum(shifted, axis=1, keepdims=True)
    wanted = jnp.sum(jnp.where(eye, positives[...], 0), axis=1, keepdims=True)
    target = (wanted == lax.broadcasted_iota(jnp.int32, (QRY, PSG), 1)).astype(f32)
    dlogits = probs - target
    logits_out[...] = logits
    dlogits_out[...] = dlogits
    weighted = dlogits * logits
    sum_q = jnp.sum(weighted, axis=1, keepdims=True)
    sum_p_row = jnp.sum(weighted, axis=0, keepdims=True)
    sum_p = jnp.concatenate(
        [
            jnp.sum(jnp.where(eye, sum_p_row[:, :QRY], 0.0), axis=1, keepdims=True),
            jnp.sum(jnp.where(eye, sum_p_row[:, QRY:], 0.0), axis=1, keepdims=True),
        ],
        axis=0,
    )

    def through(rows):
        unit_q = rows[:QRY] / norm_q
        unit_p = rows[QRY:] / norm_p
        grad_q = (
            logit_scale
            * jnp.dot(dlogits, unit_p, precision=highest, preferred_element_type=f32)
            - sum_q * unit_q
        ) / norm_q
        grad_p = (
            logit_scale
            * lax.dot_general(
                dlogits, unit_q, (((0,), (0,)), ((), ())), precision=highest,
                preferred_element_type=f32,
            )
            - sum_p * unit_p
        ) / norm_p
        return grad_q, grad_p

    grad_q, grad_p = through(scaled[...])
    scale = loss_scale * gain[...]
    d_resid[:QRY] = scale * grad_q
    d_resid[QRY:] = scale * grad_p
    grad_q, grad_p = through(total[...])
    d_attn[:QRY] = (loss_scale * grad_q).astype(bf16)
    d_attn[QRY:] = (loss_scale * grad_p).astype(bf16)


def shards(attn_out, residual, out_proj, gain, positives):
    vmem = pl.BlockSpec(memory_space=pltpu.VMEM)
    hbm = pl.BlockSpec(memory_space=pltpu.HBM)
    dma = pltpu.SemaphoreType.DMA
    gain = gain.reshape(1, W)
    total, scaled, inner = pl.pallas_call(
        main_kernel,
        out_shape=(
            jax.ShapeDtypeStruct((GROUP, W), f32),
            jax.ShapeDtypeStruct((GROUP, W), f32),
            jax.ShapeDtypeStruct((QRY, W), f32),
        ),
        in_specs=[hbm, hbm, hbm, vmem],
        out_specs=[vmem] * 3,
        scratch_shapes=[
            pltpu.VMEM((16, GROUP, W), bf16),
            pltpu.VMEM((2, NZ, 2, 64, W), bf16),
            pltpu.VMEM((16, GROUP, W), f32),
            pltpu.VMEM((2, 4, GROUP, W), bf16),
            pltpu.VMEM((2, 4, ROWS_X, W), bf16),
            pltpu.VMEM((2, 4, GROUP, W), bf16),
            pltpu.VMEM((2, 4, ROWS_X, W), bf16),
            pltpu.VMEM((8, ROWS_Y, W), bf16),
            pltpu.VMEM((8, ROWS_Y, W), bf16),
            pltpu.VMEM((ROWS_X, W), bf16),
            pltpu.VMEM((ROWS_X, W), bf16),
            pltpu.VMEM((QRY, W), f32),
            pltpu.VMEM((16, 8, W), f32),
            pltpu.VMEM((QRY, W), f32),
            dma((3, 2, 4)), dma((3, 2, 4)),
            dma, dma,
            dma((9,)), dma((9,)),
            dma, dma,
            dma((2, 2, 8)), dma((2, 2, 8)),
            dma((2, 9)), dma((2, 9)),
            dma((3, 2, 4)), dma((3, 2, 4)),
            dma((8,)), dma((8,)),
            dma, dma,
            dma((16,)), dma((16,)),
            dma((16,)), dma((16,)),
            pltpu.VMEM((GROUP, W), bf16),
            dma((3,)),
        ],
        compiler_params=pltpu.CompilerParams(
            collective_id=0, has_side_effects=True, vmem_limit_bytes=40 * 2**20
        ),
    )(attn_out, residual, out_proj, gain)
    return pl.pallas_call(
        tail_kernel,
        out_shape=(
            jax.ShapeDtypeStruct((QRY, PSG), f32),
            jax.ShapeDtypeStruct((QRY, PSG), f32),
            jax.ShapeDtypeStruct((GROUP, W), bf16),
            jax.ShapeDtypeStruct((GROUP, W), f32),
        ),
        in_specs=[vmem] * 5,
        out_specs=[vmem] * 4,
        compiler_params=pltpu.CompilerParams(vmem_limit_bytes=32 * 2**20),
    )(total, scaled, inner, gain, positives.reshape(1, QRY))


def solution(mesh):
    return jax.shard_map(
        shards,
        mesh=mesh,
        in_specs=(P("fsdp", "dp"), P("fsdp", "dp"), P("fsdp", "dp"), P("dp"), P("fsdp")),
        out_specs=(P("fsdp", None), P("fsdp", None), P("fsdp", "dp"), P("fsdp", "dp")),
        check_vma=False,
    )
```

```python
import jax
import jax.numpy as jnp
from jax import lax
from jax.experimental import pallas as pl
from jax.experimental.pallas import tpu as pltpu
from jax.sharding import PartitionSpec as P

QRY = 96
PSG = 192
GROUP = 288
W = 256
NY, NZ = 8, 16
ROWS_X = 128
ROWS_Y = GROUP - ROWS_X
SLICES = QRY // 8

logit_scale = 20.0
loss_scale = 1024.0
highest = lax.Precision.HIGHEST
f32 = jnp.float32
bf16 = jnp.bfloat16
MESH = pl.DeviceIdType.MESH


def device(y, h, l, z, k):
    return (y * 2 + h, l * 32 + z * 2 + k)


def dot_t(left, right, precision=None):
    return lax.dot_general(
        left, right, (((1,), (1,)), ((), ())), precision=precision, preferred_element_type=f32
    )


def remote(src, dst, send, recv, target):
    return pltpu.make_async_remote_copy(
        src_ref=src, dst_ref=dst, send_sem=send, recv_sem=recv, device_id=target, device_id_type=MESH
    )


ROWS = {"a": (0, ROWS_X), "p": (0, ROWS_X), "b": (ROWS_X, ROWS_Y)}


def rows_of(kind, hop, way):
    start, size = ROWS[kind]
    if hop < 3:
        return start, size
    return start + way * (size // 2), size // 2


def main_kernel(
    attn_hbm, resid_hbm, weight_hbm, gain,
    t_out, scaled_out, z_out,
    g, wp, t, so, sp, ro, rp, xs, xr, ps, pr, zpart, zin, zsum,
    ag_s, ag_r, ax_s, ax_r, bx_s, bx_r, wl_s, wl_r, wz_s, wz_r, wk_s, wk_r,
    rs_s, rs_r, rx_s, rx_r, rp_s, rp_r, z1_s, z1_r, z2_s, z2_r,
    resid, in_sem,
):
    c = lax.axis_index("dp")
    f = lax.axis_index("fsdp")
    y, h = c // 2, c % 2
    l, z, k = f // 32, (f // 2) % 16, f % 2
    across = device(y, 1 - h, l, z, k)
    beside = device(y, h, 1 - l, z, k)
    sibling = device(y, h, l, z, 1 - k)
    along = (device((y + 1) % NY, h, l, z, k), device((y + NY - 1) % NY, h, l, z, k))
    z_near = (device(y, h, l, (z + 1) % NZ, k), device(y, h, l, (z + NZ - 1) % NZ, k))
    z_far = (device(y, h, l, (z + 2) % NZ, k), device(y, h, l, (z + NZ - 2) % NZ, k))
    peers = [((c + r) % 16, f) for r in range(1, 16)]

    barrier = pltpu.get_barrier_semaphore()
    everyone = peers + [beside, sibling, *z_near, *z_far]
    for target in everyone:
        pl.semaphore_signal(barrier, inc=1, device_id=target, device_id_type=MESH)
    load_a = pltpu.make_async_copy(attn_hbm, g.at[c], in_sem.at[0])
    load_w = pltpu.make_async_copy(weight_hbm, wp.at[l, z, k], in_sem.at[1])
    load_r = pltpu.make_async_copy(resid_hbm, resid, in_sem.at[2])
    load_a.start()
    load_w.start()
    load_r.start()
    load_a.wait()
    load_w.wait()
    load_r.wait()
    pl.semaphore_wait(barrier, len(everyone))

    def slot(step, other=0):
        return ((y + step + NY) % NY) * 2 + (1 - h if other else h)

    KINDS = ("a", "b", "p")

    def ag(kind, way, hop):
        start, size = rows_of(kind, hop, way)
        block = g.at[slot(-hop if way == 0 else hop, kind == "p"), pl.ds(start, size)]
        i = KINDS.index(kind)
        return remote(block, block, ag_s.at[i, way, hop], ag_r.at[i, way, hop], along[way])

    def ag_recv(kind, way, hop):
        start, size = rows_of(kind, hop, way)
        block = g.at[slot(-hop - 1 if way == 0 else hop + 1, kind == "p"), pl.ds(start, size)]
        i = KINDS.index(kind)
        return remote(block, block, ag_s.at[i, way, hop], ag_r.at[i, way, hop], along[way])

    def ax(other=0):
        block = g.at[slot(0, other), pl.ds(0, ROWS_X)]
        return remote(block, block, ax_s, ax_r, across)

    steps = [(0, ROWS_X, ROWS_Y)]
    for d in (1, 2, 3):
        steps += [(-d, ROWS_X, ROWS_Y), (d, ROWS_X, ROWS_Y)]
    steps += [(4, ROWS_X, ROWS_Y // 2), (4, ROWS_X + ROWS_Y // 2, ROWS_Y // 2)]

    def bx(i, other=0):
        step, start, size = steps[i]
        block = g.at[slot(step, other), pl.ds(start, size)]
        return remote(block, block, bx_s.at[i], bx_r.at[i], across)

    def wz(u, way, dist):
        hop = 2 if dist % 2 == 0 else 1
        back = dist - hop
        zz = (z - back + NZ) % NZ if way == 0 else (z + back) % NZ
        block = wp.at[1 - l if u else l, zz, k]
        target = (z_far if hop == 2 else z_near)[way]
        return remote(block, block, wz_s.at[u, way, dist - 1], wz_r.at[u, way, dist - 1], target)

    def wz_recv(u, way, dist):
        zz = (z - dist + NZ) % NZ if way == 0 else (z + dist) % NZ
        block = wp.at[1 - l if u else l, zz, k]
        return remote(block, block, wz_s.at[u, way, dist - 1], wz_r.at[u, way, dist - 1], z_near[way])

    def reach(way):
        return 8 if way == 0 else 7

    def wl(u=0):
        block = wp.at[1 - l if u else l, z, k]
        return remote(block, block, wl_s, wl_r, beside)

    def wk(way, dist, core):
        zz = (z - dist + NZ) % NZ if way == 0 else (z + dist) % NZ
        block = wp.at[:, zz, core]
        return remote(block, block, wk_s.at[way, dist], wk_r.at[way, dist], sibling)

    def wz_start(u, way, stage):
        for dist in (2 * stage + 2, 2 * stage + 1):
            if dist <= reach(way):
                wz(u, way, dist).start()

    ax().start()
    wl().start()
    for way in (0, 1):
        ag("a", way, 0).start()
        wz_start(0, way, 0)
        ag("b", way, 0).start()
    bx(0).start()
    wl(1).wait_recv()
    for way in (0, 1):
        wz_start(1, way, 0)
    wk(0, 0, k).start()
    ax(1).wait_recv()
    for way in (0, 1):
        ag("p", way, 0).start()
    for hop in range(4):
        for kind in KINDS:
            for way in (0, 1):
                ag_recv(kind, way, hop).wait_recv()
                if hop < 3:
                    ag(kind, way, hop + 1).start()
                if kind == "b":
                    bx(1 + 2 * hop + way).start()
            if kind == "a":
                u = 0
            elif kind == "p":
                u = 1
            else:
                continue
            for way in (0, 1):
                if 2 * hop + 2 <= reach(way):
                    wz_recv(u, way, 2 * hop + 2).wait_recv()
                    if hop < 3:
                        wz_start(u, way, hop + 1)
        for way in (0, 1):
            for dist in (2 * hop + 1, 2 * hop + 2):
                if dist <= reach(way):
                    if dist % 2:
                        wz_recv(0, way, dist).wait_recv()
                        wz_recv(1, way, dist).wait_recv()
                    wk(way, dist, k).start()
    for i in range(9):
        bx(i, 1).wait_recv()
    wk(0, 0, 1 - k).wait_recv()
    for way in (0, 1):
        for dist in range(1, reach(way) + 1):
            wk(way, dist, 1 - k).wait_recv()

    def panel(index):
        return wp[index // 8, pl.ds(2 * (index % 8), 2)].reshape(W, W)

    total = jnp.dot(g[0], panel(0), preferred_element_type=f32)
    for j in range(1, 16):
        total = total + jnp.dot(g[j], panel(j), preferred_element_type=f32)
    scaled = (resid[...].astype(f32) + total) * gain[...]
    scaled_out[...] = scaled

    queries, passages = scaled[:QRY], scaled[QRY:]
    zpart[:, :PSG] = dot_t(queries, passages, highest)
    squares = jnp.sum(scaled * scaled, axis=1, keepdims=True)
    lane = lax.broadcasted_iota(jnp.int32, (QRY, W - PSG), 1)
    zpart[:, PSG:] = jnp.where(
        lane == 0, squares[:QRY], jnp.where(lane == 1, squares[QRY : 2 * QRY], squares[2 * QRY :])
    )

    def z1(r):
        to = (c + r) % 16
        return to, remote(
            zpart.at[pl.ds(pl.multiple_of(8 * to, 8), 8)], zin.at[c], z1_s, z1_r, (to, f)
        )

    for r in range(1, 16):
        to = (c + r) % 16

        @pl.when(to < SLICES)
        def _():
            z1(r)[1].start()

    u = (scaled * gain[...]).astype(bf16)

    def term(step, other):
        index = slot(step, other)
        t[index] = dot_t(u, panel(index))

    def rx(i):
        return remote(xs.at[i], xr.at[i], rx_s.at[i], rx_r.at[i], across)

    order = (4, 3, -3, 2, -2, 1, -1, 0)

    def x_send(step):
        i = order.index(step)
        xs[i] = t[slot(step, 1), ROWS_X:].astype(bf16)
        rx(i).start()

    def rs(kind, way, stage):
        start, size = rows_of(kind, 3 - stage, way)
        if kind == "p":
            src, dst = sp.at[way, stage, pl.ds(start, size)], rp.at[way, stage, pl.ds(start, size)]
        else:
            src, dst = so.at[way, stage, pl.ds(start, size)], ro.at[way, stage, pl.ds(start, size)]
        i = KINDS.index(kind)
        return remote(src, dst, rs_s.at[i, way, stage], rs_r.at[i, way, stage], along[way])

    def own(kind, step, start, size):
        value = t[slot(step, kind == "p"), pl.ds(start, size)]
        if kind == "b":
            value = value + xr[order.index(step), pl.ds(start - ROWS_X, size)].astype(f32)
        return value

    def rs_send(kind, way, stage):
        dist = 4 - stage
        step = 4 if dist == 4 else (dist if way == 0 else -dist)
        out = sp if kind == "p" else so
        start, size = rows_of(kind, 3 - stage, way)
        got = rp if kind == "p" else ro
        if stage == 0:
            out[way, 0, pl.ds(start, size)] = own(kind, step, start, size).astype(bf16)
        elif stage == 1:
            rs(kind, way, 0).wait_recv()
            first, part = rows_of(kind, 3, way)
            rest, _ = rows_of(kind, 3, 1 - way)
            out[way, 1, pl.ds(first, part)] = (
                own(kind, step, first, part) + got[way, 0, pl.ds(first, part)].astype(f32)
            ).astype(bf16)
            out[way, 1, pl.ds(rest, part)] = own(kind, step, rest, part).astype(bf16)
        else:
            rs(kind, way, stage - 1).wait_recv()
            out[way, stage, pl.ds(start, size)] = (
                own(kind, step, start, size) + got[way, stage - 1, pl.ds(start, size)].astype(f32)
            ).astype(bf16)
        rs(kind, way, stage).start()

    term(4, 1)
    x_send(4)
    for way in (0, 1):
        rs_send("p", way, 0)
    term(4, 0)
    for way in (0, 1):
        rs_send("a", way, 0)
    for step in order[1:]:
        term(step, 1)
        if step in (3, -3):
            x_send(step)
        term(step, 0)

    def z2(r):
        to = (c + r) % 16
        mine = zsum.at[pl.ds(pl.multiple_of(8 * c, 8), 8)]
        return remote(mine, mine, z2_s, z2_r, (to, f))

    def b_send(stage):
        dist = 4 - stage
        for way in (0, 1):
            if stage > 0:
                rx(order.index(dist if way == 0 else -dist)).wait_recv()
            elif way == 0:
                rx(0).wait_recv()
            rs_send("b", way, stage)

    def reduce_slice():
        @pl.when(c < SLICES)
        def _():
            theirs = zin.at[pl.ds(0, 15)]
            remote(theirs, theirs, z1_s, z1_r, peers[0]).wait_recv()
            zin[c] = zpart[pl.ds(pl.multiple_of(8 * c, 8), 8)]
            acc = zin[0]
            for j in range(1, 16):
                acc = acc + zin[j]
            zsum[pl.ds(pl.multiple_of(8 * c, 8), 8)] = acc
            for r in range(1, 16):
                z2(r).start()

    for stage, sends in ((1, (2, -2)), (2, (1, -1)), (3, (0,))):
        for way in (0, 1):
            rs_send("p", way, stage)
        b_send(stage - 1)
        for step in sends:
            x_send(step)
        for way in (0, 1):
            rs_send("a", way, stage)
        if stage == 1:
            reduce_slice()
    b_send(3)

    def landed(kind):
        start, size = ROWS[kind]
        got = rp if kind == "p" else ro
        for way in (0, 1):
            rs(kind, way, 3).wait_recv()
        return (
            own(kind, 0, start, size)
            + got[0, 3, pl.ds(start, size)].astype(f32)
            + got[1, 3, pl.ds(start, size)].astype(f32)
        )

    last = remote(ps, pr, rp_s, rp_r, across)
    ps[...] = landed("p").astype(bf16)
    last.start()
    a_sum = landed("a")
    rx(order.index(0)).wait_recv()
    t_out[ROWS_X:] = landed("b")
    last.wait_recv()
    t_out[:ROWS_X] = a_sum + pr[...].astype(f32)

    def slices(ref, count, send, recv):
        part = ref.at[pl.ds(0, 8 * count)]
        return remote(part, part, send, recv, peers[0])

    @pl.when(c < SLICES)
    def _():
        slices(zsum, SLICES - 1, z2_s, z2_r).wait_recv()

    @pl.when(c >= SLICES)
    def _():
        slices(zsum, SLICES, z2_s, z2_r).wait_recv()

    z_out[...] = zsum[...]

    ax().wait_send()
    wl().wait_send()
    for i in range(9):
        bx(i).wait_send()
    for way in (0, 1):
        for hop in range(4):
            for kind in KINDS:
                ag(kind, way, hop).wait_send()
                rs(kind, way, hop).wait_send()
        for dist in range(1, reach(way) + 1):
            wz(0, way, dist).wait_send()
            wz(1, way, dist).wait_send()
            wk(way, dist, k).wait_send()
    wk(0, 0, k).wait_send()
    for i in range(8):
        rx(i).wait_send()
    last.wait_send()
    @pl.when(c < SLICES)
    def _():
        slices(zpart, SLICES - 1, z1_s, z1_r).wait_send()
        theirs = zin.at[pl.ds(0, 15)]
        remote(theirs, theirs, z2_s, z2_r, peers[0]).wait_send()

    @pl.when(c >= SLICES)
    def _():
        slices(zpart, SLICES, z1_s, z1_r).wait_send()


def tail_kernel(total, scaled, inner, gain, positives, logits_out, dlogits_out, d_attn, d_resid):
    eye = lax.broadcasted_iota(jnp.int32, (QRY, QRY), 0) == lax.broadcasted_iota(
        jnp.int32, (QRY, QRY), 1
    )

    def as_row(column):
        return jnp.sum(jnp.where(eye, column, 0.0), axis=0, keepdims=True)

    norm_q = jnp.sqrt(inner[:, PSG : PSG + 1] + 1e-06)
    norm_p1 = jnp.sqrt(inner[:, PSG + 1 : PSG + 2] + 1e-06)
    norm_p2 = jnp.sqrt(inner[:, PSG + 2 : PSG + 3] + 1e-06)
    norm_p = jnp.concatenate([norm_p1, norm_p2], axis=0)
    row_p = jnp.concatenate([as_row(norm_p1), as_row(norm_p2)], axis=1)
    logits = logit_scale * inner[:, :PSG] / (norm_q * row_p)
    shifted = jnp.exp(logits - logit_scale)
    probs = shifted / jnp.sum(shifted, axis=1, keepdims=True)
    wanted = jnp.sum(jnp.where(eye, positives[...], 0), axis=1, keepdims=True)
    target = (wanted == lax.broadcasted_iota(jnp.int32, (QRY, PSG), 1)).astype(f32)
    dlogits = probs - target
    logits_out[...] = logits
    dlogits_out[...] = dlogits
    weighted = dlogits * logits
    sum_q = jnp.sum(weighted, axis=1, keepdims=True)
    sum_p_row = jnp.sum(weighted, axis=0, keepdims=True)
    sum_p = jnp.concatenate(
        [
            jnp.sum(jnp.where(eye, sum_p_row[:, :QRY], 0.0), axis=1, keepdims=True),
            jnp.sum(jnp.where(eye, sum_p_row[:, QRY:], 0.0), axis=1, keepdims=True),
        ],
        axis=0,
    )

    def through(rows):
        unit_q = rows[:QRY] / norm_q
        unit_p = rows[QRY:] / norm_p
        grad_q = (
            logit_scale
            * jnp.dot(dlogits, unit_p, precision=highest, preferred_element_type=f32)
            - sum_q * unit_q
        ) / norm_q
        grad_p = (
            logit_scale
            * lax.dot_general(
                dlogits, unit_q, (((0,), (0,)), ((), ())), precision=highest,
                preferred_element_type=f32,
            )
            - sum_p * unit_p
        ) / norm_p
        return grad_q, grad_p

    grad_q, grad_p = through(scaled[...])
    scale = loss_scale * gain[...]
    d_resid[:QRY] = scale * grad_q
    d_resid[QRY:] = scale * grad_p
    grad_q, grad_p = through(total[...])
    d_attn[:QRY] = (loss_scale * grad_q).astype(bf16)
    d_attn[QRY:] = (loss_scale * grad_p).astype(bf16)


def shards(attn_out, residual, out_proj, gain, positives):
    vmem = pl.BlockSpec(memory_space=pltpu.VMEM)
    hbm = pl.BlockSpec(memory_space=pltpu.HBM)
    dma = pltpu.SemaphoreType.DMA
    gain = gain.reshape(1, W)
    total, scaled, inner = pl.pallas_call(
        main_kernel,
        out_shape=(
            jax.ShapeDtypeStruct((GROUP, W), f32),
            jax.ShapeDtypeStruct((GROUP, W), f32),
            jax.ShapeDtypeStruct((QRY, W), f32),
        ),
        in_specs=[hbm, hbm, hbm, vmem],
        out_specs=[vmem] * 3,
        scratch_shapes=[
            pltpu.VMEM((16, GROUP, W), bf16),
            pltpu.VMEM((2, NZ, 2, 64, W), bf16),
            pltpu.VMEM((16, GROUP, W), f32),
            pltpu.VMEM((2, 4, GROUP, W), bf16),
            pltpu.VMEM((2, 4, ROWS_X, W), bf16),
            pltpu.VMEM((2, 4, GROUP, W), bf16),
            pltpu.VMEM((2, 4, ROWS_X, W), bf16),
            pltpu.VMEM((8, ROWS_Y, W), bf16),
            pltpu.VMEM((8, ROWS_Y, W), bf16),
            pltpu.VMEM((ROWS_X, W), bf16),
            pltpu.VMEM((ROWS_X, W), bf16),
            pltpu.VMEM((QRY, W), f32),
            pltpu.VMEM((16, 8, W), f32),
            pltpu.VMEM((QRY, W), f32),
            dma((3, 2, 4)), dma((3, 2, 4)),
            dma, dma,
            dma((9,)), dma((9,)),
            dma, dma,
            dma((2, 2, 8)), dma((2, 2, 8)),
            dma((2, 9)), dma((2, 9)),
            dma((3, 2, 4)), dma((3, 2, 4)),
            dma((8,)), dma((8,)),
            dma, dma,
            dma, dma,
            dma, dma,
            pltpu.VMEM((GROUP, W), bf16),
            dma((3,)),
        ],
        compiler_params=pltpu.CompilerParams(
            collective_id=0, has_side_effects=True, vmem_limit_bytes=40 * 2**20
        ),
    )(attn_out, residual, out_proj, gain)
    return pl.pallas_call(
        tail_kernel,
        out_shape=(
            jax.ShapeDtypeStruct((QRY, PSG), f32),
            jax.ShapeDtypeStruct((QRY, PSG), f32),
            jax.ShapeDtypeStruct((GROUP, W), bf16),
            jax.ShapeDtypeStruct((GROUP, W), f32),
        ),
        in_specs=[vmem] * 5,
        out_specs=[vmem] * 4,
        compiler_params=pltpu.CompilerParams(vmem_limit_bytes=32 * 2**20),
    )(total, scaled, inner, gain, positives.reshape(1, QRY))


def solution(mesh):
    return jax.shard_map(
        shards,
        mesh=mesh,
        in_specs=(P("fsdp", "dp"), P("fsdp", "dp"), P("fsdp", "dp"), P("dp"), P("fsdp")),
        out_specs=(P("fsdp", None), P("fsdp", None), P("fsdp", "dp"), P("fsdp", "dp")),
        check_vma=False,
    )
```
